32 devices in a mesh: quad: 8 (over z, x), conf: 4 (over y, core).
Axes of the slice: x: 2, y: 2, z: 4, core: 2. Of those that a mesh axis runs over, the one named last changes fastest.
Arguments:
- configs: bfloat16 [8192, 6144], P('conf', 'quad'), may hold values from -0.078125 to 0.078125
- weights: float32 [6144], P('quad'), may hold values from 0.5 to 2
Outputs:
- shell_matrix: float32 [8192, 8192], P('quad', 'conf')
The draws below stay inside these ranges and needn't reach their ends.
All inputs are finite; a program needn't handle non-finite values.
Results may differ from the reference program's by a relative error of at most 0.0085.
Values may be sent and summed in bfloat16 or wider, within the bound.
A program may use at most 128 MiB of HBM per device.

```python
import jax
import jax.numpy as jnp
from jax import lax

NCONF = 8192
NQ = 6144


def steps_of(own_key, shape, shards, least, top_value):
    level, own = 1.0, jax.random.fold_in(own_key, 6)
    for position, blocks in shards:
        draws = jnp.exp(jax.random.uniform(jax.random.fold_in(own, position), (blocks,), jnp.float32, least / len(shards), top_value / len(shards)))
        level = level * jnp.repeat(draws, shape[position] // blocks).reshape([-1 if axis == position else 1 for axis in range(len(shape))])
    return level


def bell_draw(rng, shape, width, most, pieces=(), held_as=jnp.bfloat16):
    values = jax.random.normal(rng, shape, jnp.float32) * width
    if len(pieces) > 0:
        values = steps_of(rng, shape, pieces, -0.22, 0.18) * values
    return jnp.clip(values, min=-most, max=most).astype(held_as)


def setup_inputs(seed: int = 0) -> dict:
    key_list = jax.random.split(jax.random.key(seed), 3)
    configs = bell_draw(key_list[0], (NCONF, NQ), NQ ** -0.5, 0.078125, ((0, 4), (1, 8)))
    weights = jnp.clip(0.5 + 1.5 * jax.random.uniform(key_list[1], (NQ,), jnp.float32) ** steps_of(key_list[1], (NQ,), ((0, 8),), -0.2, 0.2), 0.5, 2.0)
    return dict(configs=configs, weights=weights)


def reference(configs, weights):
    scaled = (configs.astype(jnp.float32) * weights[None, :]).astype(jnp.bfloat16)
    return lax.dot_general(scaled, configs, (((1,), (1,)), ((), ())), preferred_element_type=jnp.float32)
```

```python
import functools

import jax
import jax.numpy as jnp
from jax import lax
from jax.experimental import pallas as pl
from jax.experimental.pallas import tpu as pltpu
from jax.sharding import PartitionSpec as P

MESH = pl.DeviceIdType.MESH


def visit(z, k, nz):
    below, above = z, nz - 1 - z
    pairs = jnp.minimum(below, above)
    paired = k <= 2 * pairs
    step = jnp.where(paired, (k + 1) // 2, k - pairs)
    down = jnp.where(paired, k % 2 == 1, below > above)
    return jnp.where(down, z - step, z + step)


def kernel(nq, nc, x_ref, w_ref, out_ref, held, left, wts, scaled,
           load_sem, recv_sem, line_sem, own_sem, pair_sem, left_recv, left_send, w_recv, w_send):
    chunks, rows, _ = x_ref.shape
    nz = nq // 2
    q, c = lax.axis_index("quad"), lax.axis_index("conf")
    z, x = q // 2, q % 2
    root, mine = q // chunks, q % chunks
    bits = nc.bit_length() - 1
    far = 0
    for b in range(bits):
        far = far + (((c // 2**b) % 2 + (root // 2**b) % 2) % 2) * 2**b

    load = pltpu.make_async_copy(x_ref, held.at[q], load_sem)
    load.start()
    barrier = pltpu.get_barrier_semaphore()
    for k in range(1, nq):
        pl.semaphore_signal(barrier, inc=1, device_id={"quad": lax.rem(q + k, nq)}, device_id_type=MESH)
    for k in range(1, nc):
        pl.semaphore_signal(barrier, inc=1, device_id={"conf": lax.rem(c + k, nc)}, device_id_type=MESH)
    wts[q] = jnp.broadcast_to(w_ref[...], wts.shape[1:])
    load.wait()
    pl.semaphore_wait(barrier, nq + nc - 2)

    def along(slot, ch, to, sem):
        return pltpu.make_async_remote_copy(
            src_ref=held.at[slot, ch], dst_ref=held.at[slot, ch], send_sem=sem,
            recv_sem=recv_sem.at[slot, ch], device_id={"quad": to}, device_id_type=MESH)

    def line_copy(slot, ch, to):
        return along(slot, ch, to, line_sem.at[slot // 2, ch])

    def own_copy(ch, to):
        return along(q, ch, to, own_sem.at[ch])

    def pair_copy(slot, ch):
        return along(slot, ch, 2 * z + 1 - x, pair_sem.at[slot // 2, ch])

    def left_copy(src, slot, b):
        bit = (c // 2**b) % 2
        return pltpu.make_async_remote_copy(
            src_ref=src, dst_ref=left.at[slot], send_sem=left_send.at[slot, b],
            recv_sem=left_recv.at[slot], device_id={"conf": c + (1 - 2 * bit) * 2**b}, device_id_type=MESH)

    def weight_copy(k):
        return pltpu.make_async_remote_copy(
            src_ref=wts.at[q], dst_ref=wts.at[q], send_sem=w_send.at[k],
            recv_sem=w_recv.at[q], device_id={"quad": lax.rem(q + k, nq)}, device_id_type=MESH)

    def pass_left(src, slot, here):
        for b in reversed(range(bits)):
            @pl.when(jnp.logical_and(here, far % 2 ** (b + 1) == 0))
            def _():
                left_copy(src, slot, b).start()

    def root_sends(slot, ch):
        pass_left(held.at[slot, ch], slot, jnp.logical_and(far == 0, ch == mine))

    def turn(ch, source):
        return (ch + 1 - source) % chunks

    for i in range(chunks):
        ch = turn(i, x)

        @pl.when(z < nz - 1)
        def _():
            line_copy(q, ch, q + 2).start()

        @pl.when(z > 0)
        def _():
            own_copy(ch, q - 2).start()

        pair_copy(q, ch).start()
        root_sends(q, ch)
    for k in range(1, nq):
        weight_copy(k).start()

    out_ref[...] = jnp.zeros_like(out_ref)

    def multiply(slot):
        @pl.when(slot != q)
        def _():
            weight_copy_from = pltpu.make_async_remote_copy(
                src_ref=wts.at[slot], dst_ref=wts.at[slot], send_sem=w_send.at[0],
                recv_sem=w_recv.at[slot], device_id={"quad": lax.rem(q + 1, nq)}, device_id_type=MESH)
            weight_copy_from.wait_recv()

        scale = wts[slot, 0:1, :]

        @pl.when(far != 0)
        def _():
            left_copy(left.at[slot], slot, 0).wait_recv()
            pass_left(left.at[slot], slot, True)
            scaled[...] = (left[slot].astype(jnp.float32) * scale).astype(jnp.bfloat16)

        @pl.when(far == 0)
        def _():
            scaled[...] = (held[slot, mine].astype(jnp.float32) * scale).astype(jnp.bfloat16)

        tile = min(256, rows)
        for ch in range(chunks):
            @pl.loop(0, rows // tile)
            def _(t):
                part = pl.ds(pl.multiple_of(t * tile, tile), tile)
                out_ref[part, ch * rows:(ch + 1) * rows] += lax.dot_general(
                    scaled[part, :], held[slot, ch], (((1,), (1,)), ((), ())),
                    preferred_element_type=jnp.float32)

    @pl.loop(1, nz + 2)
    def _(k):
        at = visit(z, jnp.minimum(k, nz - 1), nz)
        slot = 2 * at + x
        before = visit(z, jnp.clip(k - 1, 0, nz - 1), nz)
        for i in range(chunks):
            @pl.when(k < nz)
            def _():
                ch = turn(i, x)
                line_copy(slot, ch, q).wait_recv()

                @pl.when(jnp.logical_and(at < z, z < nz - 1))
                def _():
                    line_copy(slot, ch, q + 2).start()

                @pl.when(jnp.logical_and(at > z, z > 0))
                def _():
                    line_copy(slot, ch, q - 2).start()

                pair_copy(slot, ch).start()
                root_sends(slot, ch)

            @pl.when(k <= nz)
            def _():
                ch = turn(i, 1 - x)
                other = 2 * before + 1 - x
                line_copy(other, ch, q).wait_recv()
                root_sends(other, ch)

        @pl.when(k <= nz)
        def _():
            multiply(2 * before + x)

        @pl.when(k >= 2)
        def _():
            multiply(2 * visit(z, jnp.maximum(k - 2, 0), nz) + 1 - x)

    for ch in range(chunks):
        @pl.when(z > 0)
        def _():
            own_copy(ch, q - 2).wait_send()

    @pl.loop(0, nz)
    def _(at):
        for ch in range(chunks):
            slot = 2 * at + x
            sent = jnp.logical_or(jnp.logical_and(at <= z, z < nz - 1), jnp.logical_and(at > z, z > 0))

            @pl.when(sent)
            def _():
                line_copy(slot, ch, q).wait_send()

            pair_copy(slot, ch).wait_send()

    @pl.loop(0, nq)
    def _(slot):
        for b in range(bits):
            @pl.when(far % 2 ** (b + 1) == 0)
            def _():
                left_copy(left.at[slot], slot, b).wait_send()

    for k in range(1, nq):
        weight_copy(k).wait_send()


def local(nq, nc, configs, weights):
    columns, width = configs.shape
    rows = columns * nc // nq
    chunks = columns // rows
    dma = pltpu.SemaphoreType.DMA
    bits = nc.bit_length() - 1
    return pl.pallas_call(
        functools.partial(kernel, nq, nc),
        out_shape=jax.ShapeDtypeStruct((rows, columns), jnp.float32),
        in_specs=[pl.BlockSpec(memory_space=pl.ANY), pl.BlockSpec(memory_space=pltpu.VMEM)],
        out_specs=pl.BlockSpec(memory_space=pltpu.VMEM),
        scratch_shapes=[
            pltpu.VMEM((nq, chunks, rows, width), jnp.bfloat16),
            pltpu.VMEM((nq, rows, width), jnp.bfloat16),
            pltpu.VMEM((nq, 8, width), jnp.float32),
            pltpu.VMEM((rows, width), jnp.bfloat16),
            dma,
            dma((nq, chunks)),
            dma((nq // 2, chunks)),
            dma((chunks,)),
            dma((nq // 2, chunks)),
            dma((nq,)),
            dma((nq, bits)),
            dma((nq,)),
            dma((nq,)),
        ],
        compiler_params=pltpu.CompilerParams(
            collective_id=0, has_side_effects=True, vmem_limit_bytes=60 * 2**20),
        cost_estimate=pl.CostEstimate(
            flops=2 * rows * columns * width * nq, transcendentals=0,
            bytes_accessed=2 * columns * width + 4 * rows * columns),
    )(configs.reshape(chunks, rows, width), weights.reshape(1, width))


def solution(mesh):
    return jax.shard_map(
        functools.partial(local, mesh.shape["quad"], mesh.shape["conf"]),
        mesh=mesh,
        in_specs=(P("conf", "quad"), P("quad")),
        out_specs=P("quad", "conf"),
        check_vma=False,
    )
```

```python
import functools

import jax
import jax.numpy as jnp
from jax import lax
from jax.experimental import pallas as pl
from jax.experimental.pallas import tpu as pltpu
from jax.sharding import PartitionSpec as P

MESH = pl.DeviceIdType.MESH


def visit(z, k, nz):
    below, above = z, nz - 1 - z
    pairs = jnp.minimum(below, above)
    paired = k <= 2 * pairs
    step = jnp.where(paired, (k + 1) // 2, k - pairs)
    down = jnp.where(paired, k % 2 == 1, below > above)
    return jnp.where(down, z - step, z + step)


def kernel(nq, nc, x_ref, w_ref, out_ref, held, left, wts, scaled,
           load_sem, recv_sem, line_sem, own_sem, pair_sem, cross_sem, left_recv, left_send, w_recv, w_send):
    chunks, rows, _ = x_ref.shape
    nz = nq // 2
    q, c = lax.axis_index("quad"), lax.axis_index("conf")
    z, x = q // 2, q % 2
    root, mine = q // chunks, q % chunks
    buddy = z + 1 - 2 * (z % 2)
    bits = nc.bit_length() - 1
    far = 0
    for b in range(bits):
        far = far + (((c // 2**b) % 2 + (root // 2**b) % 2) % 2) * 2**b

    load = pltpu.make_async_copy(x_ref, held.at[q], load_sem)
    load.start()
    barrier = pltpu.get_barrier_semaphore()
    for k in range(1, nq):
        pl.semaphore_signal(barrier, inc=1, device_id={"quad": lax.rem(q + k, nq)}, device_id_type=MESH)
    for k in range(1, nc):
        pl.semaphore_signal(barrier, inc=1, device_id={"conf": lax.rem(c + k, nc)}, device_id_type=MESH)
    wts[q] = jnp.broadcast_to(w_ref[...].reshape(1, -1), wts.shape[1:])
    load.wait()
    pl.semaphore_wait(barrier, nq + nc - 2)

    def along(slot, ch, to, sem):
        return pltpu.make_async_remote_copy(
            src_ref=held.at[slot, ch], dst_ref=held.at[slot, ch], send_sem=sem,
            recv_sem=recv_sem.at[slot, ch], device_id={"quad": to}, device_id_type=MESH)

    def line_copy(slot, ch, to):
        return along(slot, ch, to, line_sem.at[slot // 2, ch])

    def own_copy(ch, to):
        return along(q, ch, to, own_sem.at[ch])

    def pair_copy(slot, ch):
        return along(slot, ch, 2 * z + 1 - x, pair_sem.at[slot // 2, ch])

    def cross_copy(at):
        return along(2 * at + 1 - x, turn(chunks - 1, 1 - x), 2 * buddy + x, cross_sem)

    def left_copy(src, slot, b):
        bit = (c // 2**b) % 2
        return pltpu.make_async_remote_copy(
            src_ref=src, dst_ref=left.at[slot], send_sem=left_send.at[slot, b],
            recv_sem=left_recv.at[slot], device_id={"conf": c + (1 - 2 * bit) * 2**b}, device_id_type=MESH)

    def weight_copy(k):
        return pltpu.make_async_remote_copy(
            src_ref=wts.at[q], dst_ref=wts.at[q], send_sem=w_send.at[k],
            recv_sem=w_recv.at[q], device_id={"quad": lax.rem(q + k, nq)}, device_id_type=MESH)

    def pass_left(src, slot, here):
        for b in reversed(range(bits)):
            @pl.when(jnp.logical_and(here, far % 2 ** (b + 1) == 0))
            def _():
                left_copy(src, slot, b).start()

    def root_sends(slot, ch):
        pass_left(held.at[slot, ch], slot, jnp.logical_and(far == 0, ch == mine))

    def turn(ch, source):
        return (ch + 1 - source) % chunks

    for i in range(chunks):
        ch = turn(i, x)

        @pl.when(z < nz - 1)
        def _():
            line_copy(q, ch, q + 2).start()

        @pl.when(z > 0)
        def _():
            own_copy(ch, q - 2).start()

        pair_copy(q, ch).start()
        root_sends(q, ch)
    for k in range(1, nq):
        weight_copy(k).start()

    out_ref[...] = jnp.zeros_like(out_ref)

    def multiply(slot):
        @pl.when(slot != q)
        def _():
            weight_copy_from = pltpu.make_async_remote_copy(
                src_ref=wts.at[slot], dst_ref=wts.at[slot], send_sem=w_send.at[0],
                recv_sem=w_recv.at[slot], device_id={"quad": lax.rem(q + 1, nq)}, device_id_type=MESH)
            weight_copy_from.wait_recv()

        scale = wts[slot, 0:1, :]

        @pl.when(far != 0)
        def _():
            left_copy(left.at[slot], slot, 0).wait_recv()
            pass_left(left.at[slot], slot, True)
            scaled[...] = (left[slot].astype(jnp.float32) * scale).astype(jnp.bfloat16)

        @pl.when(far == 0)
        def _():
            scaled[...] = (held[slot, mine].astype(jnp.float32) * scale).astype(jnp.bfloat16)

        tile = min(256, rows)
        for ch in range(chunks):
            @pl.loop(0, rows // tile)
            def _(t):
                part = pl.ds(pl.multiple_of(t * tile, tile), tile)
                out_ref[part, ch * rows:(ch + 1) * rows] += lax.dot_general(
                    scaled[part, :], held[slot, ch], (((1,), (1,)), ((), ())),
                    preferred_element_type=jnp.float32)

    def paired(at, i):
        return jnp.logical_or(at != buddy, i < chunks - 1)

    @pl.loop(1, nz + 2)
    def _(k):
        at = visit(z, jnp.minimum(k, nz - 1), nz)
        slot = 2 * at + x
        before = visit(z, jnp.clip(k - 1, 0, nz - 1), nz)
        for i in range(chunks):
            @pl.when(k < nz)
            def _():
                ch = turn(i, x)
                line_copy(slot, ch, q).wait_recv()

                @pl.when(jnp.logical_and(at < z, z < nz - 1))
                def _():
                    line_copy(slot, ch, q + 2).start()

                @pl.when(jnp.logical_and(at > z, z > 0))
                def _():
                    line_copy(slot, ch, q - 2).start()

                @pl.when(paired(at, i))
                def _():
                    pair_copy(slot, ch).start()

                root_sends(slot, ch)

            @pl.when(jnp.logical_and(k <= nz, paired(before, i)))
            def _():
                ch = turn(i, 1 - x)
                other = 2 * before + 1 - x
                line_copy(other, ch, q).wait_recv()
                root_sends(other, ch)

            if i == 0:
                @pl.when(k == nz)
                def _():
                    cross_copy(z).start()

        @pl.when(k <= nz)
        def _():
            multiply(2 * before + x)

        last = visit(z, jnp.maximum(k - 2, 0), nz)

        @pl.when(jnp.logical_and(k >= 2, last != buddy))
        def _():
            multiply(2 * last + 1 - x)

    other = 2 * buddy + 1 - x
    cross_copy(buddy).wait_recv()
    root_sends(other, turn(chunks - 1, 1 - x))
    multiply(other)
    cross_copy(z).wait_send()

    for ch in range(chunks):
        @pl.when(z > 0)
        def _():
            own_copy(ch, q - 2).wait_send()

    @pl.loop(0, nz)
    def _(at):
        for i in range(chunks):
            ch = turn(i, x)
            slot = 2 * at + x
            sent = jnp.logical_or(jnp.logical_and(at <= z, z < nz - 1), jnp.logical_and(at > z, z > 0))

            @pl.when(sent)
            def _():
                line_copy(slot, ch, q).wait_send()

            @pl.when(paired(at, i))
            def _():
                pair_copy(slot, ch).wait_send()

    @pl.loop(0, nq)
    def _(slot):
        for b in range(bits):
            @pl.when(far % 2 ** (b + 1) == 0)
            def _():
                left_copy(left.at[slot], slot, b).wait_send()

    for k in range(1, nq):
        weight_copy(k).wait_send()


def local(nq, nc, configs, weights):
    columns, width = configs.shape
    rows = columns * nc // nq
    chunks = columns // rows
    dma = pltpu.SemaphoreType.DMA
    bits = nc.bit_length() - 1
    return pl.pallas_call(
        functools.partial(kernel, nq, nc),
        out_shape=jax.ShapeDtypeStruct((rows, columns), jnp.float32),
        in_specs=[pl.BlockSpec(memory_space=pl.ANY), pl.BlockSpec(memory_space=pltpu.VMEM)],
        out_specs=pl.BlockSpec(memory_space=pltpu.VMEM),
        scratch_shapes=[
            pltpu.VMEM((nq, chunks, rows, width), jnp.bfloat16),
            pltpu.VMEM((nq, rows, width), jnp.bfloat16),
            pltpu.VMEM((nq, 8, width), jnp.float32),
            pltpu.VMEM((rows, width), jnp.bfloat16),
            dma,
            dma((nq, chunks)),
            dma((nq // 2, chunks)),
            dma((chunks,)),
            dma((nq // 2, chunks)),
            dma,
            dma((nq,)),
            dma((nq, bits)),
            dma((nq,)),
            dma((nq,)),
        ],
        compiler_params=pltpu.CompilerParams(
            collective_id=0, has_side_effects=True, vmem_limit_bytes=60 * 2**20),
        cost_estimate=pl.CostEstimate(
            flops=2 * rows * columns * width * nq, transcendentals=0,
            bytes_accessed=2 * columns * width + 4 * rows * columns),
    )(configs.reshape(chunks, rows, width), weights)


def solution(mesh):
    return jax.shard_map(
        functools.partial(local, mesh.shape["quad"], mesh.shape["conf"]),
        mesh=mesh,
        in_specs=(P("conf", "quad"), P("quad")),
        out_specs=P("quad", "conf"),
        check_vma=False,
    )
```

```python
import functools

import jax
import jax.numpy as jnp
from jax import lax
from jax.experimental import pallas as pl
from jax.experimental.pallas import tpu as pltpu
from jax.sharding import PartitionSpec as P

MESH = pl.DeviceIdType.MESH


def visit(z, k, nz):
    below, above = z, nz - 1 - z
    pairs = jnp.minimum(below, above)
    paired = k <= 2 * pairs
    step = jnp.where(paired, (k + 1) // 2, k - pairs)
    down = jnp.where(paired, k % 2 == 1, below > above)
    return jnp.where(down, z - step, z + step)


def kernel(nq, nc, x_ref, w_ref, out_ref, held, left, wts, scaled,
           load_sem, recv_sem, line_sem, own_sem, pair_sem, cross_sem, left_recv, left_send, w_recv, w_send):
    chunks, rows, _ = x_ref.shape
    nz = nq // 2
    q, c = lax.axis_index("quad"), lax.axis_index("conf")
    z, x = q // 2, q % 2
    root, mine = q // chunks, q % chunks
    buddy = z + 1 - 2 * (z % 2)
    bits = nc.bit_length() - 1
    far = 0
    for b in range(bits):
        far = far + (((c // 2**b) % 2 + (root // 2**b) % 2) % 2) * 2**b

    load = pltpu.make_async_copy(x_ref, held.at[q], load_sem)
    load.start()
    barrier = pltpu.get_barrier_semaphore()
    for k in range(1, nq):
        pl.semaphore_signal(barrier, inc=1, device_id={"quad": lax.rem(q + k, nq)}, device_id_type=MESH)
    for k in range(1, nc):
        pl.semaphore_signal(barrier, inc=1, device_id={"conf": lax.rem(c + k, nc)}, device_id_type=MESH)
    wts[q] = jnp.broadcast_to(w_ref[...].reshape(1, -1), wts.shape[1:])
    load.wait()
    pl.semaphore_wait(barrier, nq + nc - 2)

    parts, half = 2 * chunks, rows // 2

    def view(ref, sub):
        return ref.at[pl.ds(sub * half, half)]

    def turn(i, source):
        return (i // 2 + 1 - source) % chunks

    def along(slot, i, source, to, sem):
        block = view(held.at[slot, turn(i, source)], i % 2)
        return pltpu.make_async_remote_copy(
            src_ref=block, dst_ref=block, send_sem=sem,
            recv_sem=recv_sem.at[slot, i], device_id={"quad": to}, device_id_type=MESH)

    def line_copy(at, i, to):
        return along(2 * at + x, i, x, to, line_sem.at[at, i])

    def own_copy(i, to):
        return along(q, i, x, to, own_sem.at[i])

    def pair_copy(at, i):
        return along(2 * at + x, i, x, 2 * z + 1 - x, pair_sem.at[at, i])

    def cross_copy(at, i):
        return along(2 * at + 1 - x, i, 1 - x, 2 * buddy + x, cross_sem.at[i - parts // 2])

    def paired(at, i):
        return jnp.logical_or(at != buddy, i < parts // 2)

    def left_copy(src, slot, sub, b):
        bit = (c // 2**b) % 2
        return pltpu.make_async_remote_copy(
            src_ref=view(src, sub), dst_ref=view(left.at[slot], sub), send_sem=left_send.at[slot, sub, b],
            recv_sem=left_recv.at[slot, sub], device_id={"conf": c + (1 - 2 * bit) * 2**b}, device_id_type=MESH)

    def weight_copy(k):
        return pltpu.make_async_remote_copy(
            src_ref=wts.at[q], dst_ref=wts.at[q], send_sem=w_send.at[k],
            recv_sem=w_recv.at[q], device_id={"quad": lax.rem(q + k, nq)}, device_id_type=MESH)

    def pass_left(src, slot, sub, here):
        for b in reversed(range(bits)):
            @pl.when(jnp.logical_and(here, far % 2 ** (b + 1) == 0))
            def _():
                left_copy(src, slot, sub, b).start()

    def root_sends(slot, i, source):
        ch = turn(i, source)
        pass_left(held.at[slot, ch], slot, i % 2, jnp.logical_and(far == 0, ch == mine))

    for i in range(parts):
        @pl.when(z < nz - 1)
        def _():
            line_copy(z, i, q + 2).start()

        @pl.when(z > 0)
        def _():
            own_copy(i, q - 2).start()

        pair_copy(z, i).start()
        root_sends(q, i, x)
    for k in range(1, nq):
        weight_copy(k).start()

    out_ref[...] = jnp.zeros_like(out_ref)

    def multiply(slot, ch=None, again=False):
        if not again:
            @pl.when(slot != q)
            def _():
                pltpu.make_async_remote_copy(
                    src_ref=wts.at[slot], dst_ref=wts.at[slot], send_sem=w_send.at[0],
                    recv_sem=w_recv.at[slot], device_id={"quad": lax.rem(q + 1, nq)},
                    device_id_type=MESH).wait_recv()

            @pl.when(far != 0)
            def _():
                for sub in range(2):
                    left_copy(left.at[slot], slot, sub, 0).wait_recv()
                    pass_left(left.at[slot], slot, sub, True)

        scale = wts[slot, 0:1, :]

        @pl.when(far != 0)
        def _():
            scaled[...] = (left[slot].astype(jnp.float32) * scale).astype(jnp.bfloat16)

        @pl.when(far == 0)
        def _():
            scaled[...] = (held[slot, mine].astype(jnp.float32) * scale).astype(jnp.bfloat16)

        tile = min(256, rows)
        for block in range(chunks) if ch is None else [ch]:
            across = pl.ds(pl.multiple_of(block * rows, rows), rows)

            @pl.loop(0, rows // tile)
            def _(t):
                part = pl.ds(pl.multiple_of(t * tile, tile), tile)
                out_ref[part, across] += lax.dot_general(
                    scaled[part, :], held[slot, block], (((1,), (1,)), ((), ())),
                    preferred_element_type=jnp.float32)

    def take_line(at, i):
        line_copy(at, i, q).wait_recv()

        @pl.when(jnp.logical_and(at < z, z < nz - 1))
        def _():
            line_copy(at, i, q + 2).start()

        @pl.when(jnp.logical_and(at > z, z > 0))
        def _():
            line_copy(at, i, q - 2).start()

        @pl.when(paired(at, i))
        def _():
            pair_copy(at, i).start()

        root_sends(2 * at + x, i, x)

    def take_pair(at, i):
        @pl.when(paired(at, i))
        def _():
            along(2 * at + 1 - x, i, 1 - x, q, cross_sem.at[0]).wait_recv()
            root_sends(2 * at + 1 - x, i, 1 - x)

    def multiply_other(at):
        @pl.when(at != buddy)
        def _():
            multiply(2 * at + 1 - x)

    @pl.loop(1, nz)
    def _(k):
        at, before = visit(z, k, nz), visit(z, k - 1, nz)
        for i in range(parts):
            take_line(at, i)
            take_pair(before, i)
        multiply(2 * before + x)

        @pl.when(k >= 2)
        def _():
            multiply_other(visit(z, jnp.maximum(k - 2, 0), nz))

    end = visit(z, nz - 1, nz)
    for i in range(parts // 2):
        take_pair(end, i)
    for i in range(parts // 2, parts):
        cross_copy(z, i).start()
    multiply(2 * end + x)
    multiply_other(visit(z, nz - 2, nz))

    last, crossed = 2 * end + 1 - x, 2 * buddy + 1 - x
    split = chunks == 2 and nz > 2
    if split:
        multiply(crossed, turn(0, 1 - x))
        multiply(last, turn(0, 1 - x))
    for i in range(parts // 2, parts):
        take_pair(end, i)
    if split:
        multiply(last, turn(parts - 1, 1 - x), again=True)
    else:
        multiply_other(end)
    for i in range(parts // 2, parts):
        cross_copy(buddy, i).wait_recv()
        root_sends(crossed, i, 1 - x)
    if split:
        multiply(crossed, turn(parts - 1, 1 - x), again=True)
    else:
        multiply(crossed)

    for i in range(parts // 2, parts):
        cross_copy(z, i).wait_send()

    for i in range(parts):
        @pl.when(z > 0)
        def _():
            own_copy(i, q - 2).wait_send()

    @pl.loop(0, nz)
    def _(at):
        sent = jnp.logical_or(jnp.logical_and(at <= z, z < nz - 1), jnp.logical_and(at > z, z > 0))
        for i in range(parts):
            @pl.when(sent)
            def _():
                line_copy(at, i, q).wait_send()

            @pl.when(paired(at, i))
            def _():
                pair_copy(at, i).wait_send()

    @pl.loop(0, nq)
    def _(slot):
        for b in range(bits):
            @pl.when(far % 2 ** (b + 1) == 0)
            def _():
                for sub in range(2):
                    left_copy(left.at[slot], slot, sub, b).wait_send()

    for k in range(1, nq):
        weight_copy(k).wait_send()


def local(nq, nc, configs, weights):
    columns, width = configs.shape
    rows = columns * nc // nq
    chunks = columns // rows
    dma = pltpu.SemaphoreType.DMA
    bits = nc.bit_length() - 1
    return pl.pallas_call(
        functools.partial(kernel, nq, nc),
        out_shape=jax.ShapeDtypeStruct((rows, columns), jnp.float32),
        in_specs=[pl.BlockSpec(memory_space=pl.ANY), pl.BlockSpec(memory_space=pltpu.VMEM)],
        out_specs=pl.BlockSpec(memory_space=pltpu.VMEM),
        scratch_shapes=[
            pltpu.VMEM((nq, chunks, rows, width), jnp.bfloat16),
            pltpu.VMEM((nq, rows, width), jnp.bfloat16),
            pltpu.VMEM((nq, 8, width), jnp.float32),
            pltpu.VMEM((rows, width), jnp.bfloat16),
            dma,
            dma((nq, 2 * chunks)),
            dma((nq // 2, 2 * chunks)),
            dma((2 * chunks,)),
            dma((nq // 2, 2 * chunks)),
            dma((chunks,)),
            dma((nq, 2)),
            dma((nq, 2, bits)),
            dma((nq,)),
            dma((nq,)),
        ],
        compiler_params=pltpu.CompilerParams(
            collective_id=0, has_side_effects=True, vmem_limit_bytes=60 * 2**20),
        cost_estimate=pl.CostEstimate(
            flops=2 * rows * columns * width * nq, transcendentals=0,
            bytes_accessed=2 * columns * width + 4 * rows * columns),
    )(configs.reshape(chunks, rows, width), weights)


def solution(mesh):
    return jax.shard_map(
        functools.partial(local, mesh.shape["quad"], mesh.shape["conf"]),
        mesh=mesh,
        in_specs=(P("conf", "quad"), P("quad")),
        out_specs=P("quad", "conf"),
        check_vma=False,
    )
```

```python
import functools

import jax
import jax.numpy as jnp
from jax import lax
from jax.experimental import pallas as pl
from jax.experimental.pallas import tpu as pltpu
from jax.sharding import PartitionSpec as P

MESH = pl.DeviceIdType.MESH


def visit(z, k, nz):
    below, above = z, nz - 1 - z
    pairs = jnp.minimum(below, above)
    paired = k <= 2 * pairs
    step = jnp.where(paired, (k + 1) // 2, k - pairs)
    down = jnp.where(paired, k % 2 == 1, below > above)
    return jnp.where(down, z - step, z + step)


def kernel(nq, nc, x_ref, w_ref, out_ref, held, left, wts, scaled,
           load_sem, recv_sem, line_sem, own_sem, pair_sem, cross_sem, left_recv, left_send, w_recv, w_send):
    chunks, rows, _ = x_ref.shape
    nz = nq // 2
    q, c = lax.axis_index("quad"), lax.axis_index("conf")
    z, x = q // 2, q % 2
    root, mine = q // chunks, q % chunks
    buddy = z + 1 - 2 * (z % 2)
    bits = nc.bit_length() - 1
    far = 0
    for b in range(bits):
        far = far + (((c // 2**b) % 2 + (root // 2**b) % 2) % 2) * 2**b

    load = pltpu.make_async_copy(x_ref, held.at[q], load_sem)
    load.start()
    barrier = pltpu.get_barrier_semaphore()
    for k in range(1, nq):
        pl.semaphore_signal(barrier, inc=1, device_id={"quad": lax.rem(q + k, nq)}, device_id_type=MESH)
    for k in range(1, nc):
        pl.semaphore_signal(barrier, inc=1, device_id={"conf": lax.rem(c + k, nc)}, device_id_type=MESH)
    wts[q] = jnp.broadcast_to(w_ref[...].reshape(1, -1), wts.shape[1:])
    load.wait()
    pl.semaphore_wait(barrier, nq + nc - 2)

    parts, half = 2 * chunks, rows // 2

    def view(ref, sub):
        return ref.at[pl.ds(sub * half, half)]

    def turn(i, source):
        return (i // 2 + 1 - source) % chunks

    def along(slot, i, source, to, sem):
        block = view(held.at[slot, turn(i, source)], i % 2)
        return pltpu.make_async_remote_copy(
            src_ref=block, dst_ref=block, send_sem=sem,
            recv_sem=recv_sem.at[slot, i], device_id={"quad": to}, device_id_type=MESH)

    def line_copy(at, i, to):
        return along(2 * at + x, i, x, to, line_sem.at[at, i])

    def own_copy(i, to):
        return along(q, i, x, to, own_sem.at[i])

    def pair_copy(at, i):
        return along(2 * at + x, i, x, 2 * z + 1 - x, pair_sem.at[at, i])

    def cross_copy(at, i):
        return along(2 * at + 1 - x, i, 1 - x, 2 * buddy + x, cross_sem.at[i])

    def paired(at, i):
        return jnp.logical_or(at != buddy, jnp.logical_and(i < parts // 2, jnp.logical_not(at_end(buddy))))

    def at_end(at):
        return jnp.logical_or(at == 0, at == nz - 1)

    def left_copy(src, slot, sub, b):
        bit = (c // 2**b) % 2
        return pltpu.make_async_remote_copy(
            src_ref=view(src, sub), dst_ref=view(left.at[slot], sub), send_sem=left_send.at[slot, sub, b],
            recv_sem=left_recv.at[slot, sub], device_id={"conf": c + (1 - 2 * bit) * 2**b}, device_id_type=MESH)

    def weight_copy(k):
        return pltpu.make_async_remote_copy(
            src_ref=wts.at[q], dst_ref=wts.at[q], send_sem=w_send.at[k],
            recv_sem=w_recv.at[q], device_id={"quad": lax.rem(q + k, nq)}, device_id_type=MESH)

    def pass_left(src, slot, sub, here):
        for b in reversed(range(bits)):
            @pl.when(jnp.logical_and(here, far % 2 ** (b + 1) == 0))
            def _():
                left_copy(src, slot, sub, b).start()

    def root_sends(slot, i, source):
        ch = turn(i, source)
        pass_left(held.at[slot, ch], slot, i % 2, jnp.logical_and(far == 0, ch == mine))

    for i in range(parts):
        @pl.when(z < nz - 1)
        def _():
            line_copy(z, i, q + 2).start()

        @pl.when(z > 0)
        def _():
            own_copy(i, q - 2).start()

        pair_copy(z, i).start()
        root_sends(q, i, x)
    for k in range(1, nq):
        weight_copy(k).start()

    out_ref[...] = jnp.zeros_like(out_ref)

    def multiply(slot, ch=None, again=False):
        if not again:
            @pl.when(slot != q)
            def _():
                pltpu.make_async_remote_copy(
                    src_ref=wts.at[slot], dst_ref=wts.at[slot], send_sem=w_send.at[0],
                    recv_sem=w_recv.at[slot], device_id={"quad": lax.rem(q + 1, nq)},
                    device_id_type=MESH).wait_recv()

            @pl.when(far != 0)
            def _():
                for sub in range(2):
                    left_copy(left.at[slot], slot, sub, 0).wait_recv()
                    pass_left(left.at[slot], slot, sub, True)

        scale = wts[slot, 0:1, :]

        @pl.when(far != 0)
        def _():
            scaled[...] = (left[slot].astype(jnp.float32) * scale).astype(jnp.bfloat16)

        @pl.when(far == 0)
        def _():
            scaled[...] = (held[slot, mine].astype(jnp.float32) * scale).astype(jnp.bfloat16)

        tile = min(256, rows)
        for block in range(chunks) if ch is None else [ch]:
            across = pl.ds(pl.multiple_of(block * rows, rows), rows)

            @pl.loop(0, rows // tile)
            def _(t):
                part = pl.ds(pl.multiple_of(t * tile, tile), tile)
                out_ref[part, across] += lax.dot_general(
                    scaled[part, :], held[slot, block], (((1,), (1,)), ((), ())),
                    preferred_element_type=jnp.float32)

    def take_line(at, i):
        line_copy(at, i, q).wait_recv()

        @pl.when(jnp.logical_and(at < z, z < nz - 1))
        def _():
            line_copy(at, i, q + 2).start()

        @pl.when(jnp.logical_and(at > z, z > 0))
        def _():
            line_copy(at, i, q - 2).start()

        @pl.when(paired(at, i))
        def _():
            pair_copy(at, i).start()

        root_sends(2 * at + x, i, x)

    def take_pair(at, i):
        @pl.when(paired(at, i))
        def _():
            along(2 * at + 1 - x, i, 1 - x, q, cross_sem.at[0]).wait_recv()
            root_sends(2 * at + 1 - x, i, 1 - x)

    def multiply_other(at):
        @pl.when(at != buddy)
        def _():
            multiply(2 * at + 1 - x)

    @pl.loop(1, nz)
    def _(k):
        at, before = visit(z, k, nz), visit(z, k - 1, nz)
        for i in range(parts):
            take_line(at, i)
            take_pair(before, i)
            if i == parts // 2 - 1:
                multiply(2 * before + x)

                @pl.when(k >= 2)
                def _():
                    multiply_other(visit(z, jnp.maximum(k - 2, 0), nz))

        @pl.when(jnp.logical_and(k == 1, at_end(z)))
        def _():
            for i in range(parts):
                cross_copy(z, i).start()

    end = visit(z, nz - 1, nz)
    for i in range(parts // 2):
        take_pair(end, i)

    @pl.when(jnp.logical_not(at_end(z)))
    def _():
        for i in range(parts // 2, parts):
            cross_copy(z, i).start()

    multiply(2 * end + x)
    multiply_other(visit(z, nz - 2, nz))

    last, crossed = 2 * end + 1 - x, 2 * buddy + 1 - x
    split = chunks == 2 and nz > 2

    @pl.when(at_end(buddy))
    def _():
        for i in range(parts // 2):
            cross_copy(buddy, i).wait_recv()
            root_sends(crossed, i, 1 - x)

    if split:
        multiply(crossed, turn(0, 1 - x))
        multiply(last, turn(0, 1 - x))
    for i in range(parts // 2, parts):
        take_pair(end, i)
    if split:
        multiply(last, turn(parts - 1, 1 - x), again=True)
    else:
        multiply_other(end)
    for i in range(parts // 2, parts):
        cross_copy(buddy, i).wait_recv()
        root_sends(crossed, i, 1 - x)
    if split:
        multiply(crossed, turn(parts - 1, 1 - x), again=True)
    else:
        multiply(crossed)

    for i in range(parts):
        @pl.when(jnp.logical_or(i >= parts // 2, at_end(z)))
        def _():
            cross_copy(z, i).wait_send()

    for i in range(parts):
        @pl.when(z > 0)
        def _():
            own_copy(i, q - 2).wait_send()

    @pl.loop(0, nz)
    def _(at):
        sent = jnp.logical_or(jnp.logical_and(at <= z, z < nz - 1), jnp.logical_and(at > z, z > 0))
        for i in range(parts):
            @pl.when(sent)
            def _():
                line_copy(at, i, q).wait_send()

            @pl.when(paired(at, i))
            def _():
                pair_copy(at, i).wait_send()

    @pl.loop(0, nq)
    def _(slot):
        for b in range(bits):
            @pl.when(far % 2 ** (b + 1) == 0)
            def _():
                for sub in range(2):
                    left_copy(left.at[slot], slot, sub, b).wait_send()

    for k in range(1, nq):
        weight_copy(k).wait_send()


def local(nq, nc, configs, weights):
    columns, width = configs.shape
    rows = columns * nc // nq
    chunks = columns // rows
    dma = pltpu.SemaphoreType.DMA
    bits = nc.bit_length() - 1
    return pl.pallas_call(
        functools.partial(kernel, nq, nc),
        out_shape=jax.ShapeDtypeStruct((rows, columns), jnp.float32),
        in_specs=[pl.BlockSpec(memory_space=pl.ANY), pl.BlockSpec(memory_space=pltpu.VMEM)],
        out_specs=pl.BlockSpec(memory_space=pltpu.VMEM),
        scratch_shapes=[
            pltpu.VMEM((nq, chunks, rows, width), jnp.bfloat16),
            pltpu.VMEM((nq, rows, width), jnp.bfloat16),
            pltpu.VMEM((nq, 8, width), jnp.float32),
            pltpu.VMEM((rows, width), jnp.bfloat16),
            dma,
            dma((nq, 2 * chunks)),
            dma((nq // 2, 2 * chunks)),
            dma((2 * chunks,)),
            dma((nq // 2, 2 * chunks)),
            dma((2 * chunks,)),
            dma((nq, 2)),
            dma((nq, 2, bits)),
            dma((nq,)),
            dma((nq,)),
        ],
        compiler_params=pltpu.CompilerParams(
            collective_id=0, has_side_effects=True, vmem_limit_bytes=60 * 2**20),
        cost_estimate=pl.CostEstimate(
            flops=2 * rows * columns * width * nq, transcendentals=0,
            bytes_accessed=2 * columns * width + 4 * rows * columns),
    )(configs.reshape(chunks, rows, width), weights)


def solution(mesh):
    return jax.shard_map(
        functools.partial(local, mesh.shape["quad"], mesh.shape["conf"]),
        mesh=mesh,
        in_specs=(P("conf", "quad"), P("quad")),
        out_specs=P("quad", "conf"),
        check_vma=False,
    )
```

```python
import functools

import jax
import jax.numpy as jnp
from jax import lax
from jax.experimental import pallas as pl
from jax.experimental.pallas import tpu as pltpu
from jax.sharding import PartitionSpec as P

MESH = pl.DeviceIdType.MESH


def visit(z, k, nz):
    below, above = z, nz - 1 - z
    pairs = jnp.minimum(below, above)
    paired = k <= 2 * pairs
    step = jnp.where(paired, (k + 1) // 2, k - pairs)
    down = jnp.where(paired, k % 2 == 1, below > above)
    return jnp.where(down, z - step, z + step)


def kernel(nq, nc, x_ref, w_ref, out_ref, held, left, wts, scaled,
           load_sem, recv_sem, line_sem, own_sem, pair_sem, cross_sem, left_recv, left_send, w_recv, w_send):
    chunks, rows, _ = x_ref.shape
    nz = nq // 2
    q, c = lax.axis_index("quad"), lax.axis_index("conf")
    z, x = q // 2, q % 2
    root, mine = q // chunks, q % chunks
    buddy = z + 1 - 2 * (z % 2)
    bits = nc.bit_length() - 1
    far = 0
    for b in range(bits):
        far = far + (((c // 2**b) % 2 + (root // 2**b) % 2) % 2) * 2**b

    load = pltpu.make_async_copy(x_ref, held.at[q], load_sem)
    load.start()
    barrier = pltpu.get_barrier_semaphore()
    for k in range(1, nq):
        pl.semaphore_signal(barrier, inc=1, device_id={"quad": lax.rem(q + k, nq)}, device_id_type=MESH)
    for k in range(1, nc):
        pl.semaphore_signal(barrier, inc=1, device_id={"conf": lax.rem(c + k, nc)}, device_id_type=MESH)
    wts[q] = jnp.broadcast_to(w_ref[...].reshape(1, -1), wts.shape[1:])
    load.wait()
    pl.semaphore_wait(barrier, nq + nc - 2)

    parts, half = 2 * chunks, rows // 2

    def view(ref, sub):
        return ref.at[pl.ds(sub * half, half)]

    def turn(i, source):
        return (i // 2 + 1 - source) % chunks

    def along(slot, i, source, to, sem):
        block = view(held.at[slot, turn(i, source)], i % 2)
        return pltpu.make_async_remote_copy(
            src_ref=block, dst_ref=block, send_sem=sem,
            recv_sem=recv_sem.at[slot, i], device_id={"quad": to}, device_id_type=MESH)

    def line_copy(at, i, to):
        return along(2 * at + x, i, x, to, line_sem.at[at, i])

    def own_copy(i, to):
        return along(q, i, x, to, own_sem.at[i])

    def pair_copy(at, i):
        return along(2 * at + x, i, x, 2 * z + 1 - x, pair_sem.at[at, i])

    def cross_copy(at, i):
        return along(2 * at + 1 - x, i, 1 - x, 2 * buddy + x, cross_sem.at[i])

    def paired(at, i):
        return jnp.logical_or(at != buddy, jnp.logical_and(i < parts // 2, jnp.logical_not(at_end(buddy))))

    def at_end(at):
        return jnp.logical_or(at == 0, at == nz - 1)

    def left_copy(src, slot, sub, b):
        bit = (c // 2**b) % 2
        return pltpu.make_async_remote_copy(
            src_ref=view(src, sub), dst_ref=view(left.at[slot], sub), send_sem=left_send.at[slot, sub, b],
            recv_sem=left_recv.at[slot, sub], device_id={"conf": c + (1 - 2 * bit) * 2**b}, device_id_type=MESH)

    def weight_copy(k):
        return pltpu.make_async_remote_copy(
            src_ref=wts.at[q], dst_ref=wts.at[q], send_sem=w_send.at[k],
            recv_sem=w_recv.at[q], device_id={"quad": lax.rem(q + k, nq)}, device_id_type=MESH)

    def pass_left(src, slot, sub, here):
        for b in reversed(range(bits)):
            @pl.when(jnp.logical_and(here, far % 2 ** (b + 1) == 0))
            def _():
                left_copy(src, slot, sub, b).start()

    def root_sends(slot, i, source):
        ch = turn(i, source)
        pass_left(held.at[slot, ch], slot, i % 2, jnp.logical_and(far == 0, ch == mine))

    for i in range(parts):
        @pl.when(z < nz - 1)
        def _():
            line_copy(z, i, q + 2).start()

        @pl.when(z > 0)
        def _():
            own_copy(i, q - 2).start()

        pair_copy(z, i).start()
        root_sends(q, i, x)
    for k in range(1, nq):
        weight_copy(k).start()

    out_ref[...] = jnp.zeros_like(out_ref)

    def multiply(slot, ch=None, again=False, keep=0):
        if not again:
            @pl.when(slot != q)
            def _():
                pltpu.make_async_remote_copy(
                    src_ref=wts.at[slot], dst_ref=wts.at[slot], send_sem=w_send.at[0],
                    recv_sem=w_recv.at[slot], device_id={"quad": lax.rem(q + 1, nq)},
                    device_id_type=MESH).wait_recv()

            @pl.when(far != 0)
            def _():
                for sub in range(2):
                    left_copy(left.at[slot], slot, sub, 0).wait_recv()
                    pass_left(left.at[slot], slot, sub, True)

        scale = wts[slot, 0:1, :]

        @pl.when(jnp.logical_and(far != 0, not again))
        def _():
            scaled[keep] = (left[slot].astype(jnp.float32) * scale).astype(jnp.bfloat16)

        @pl.when(jnp.logical_and(far == 0, not again))
        def _():
            scaled[keep] = (held[slot, mine].astype(jnp.float32) * scale).astype(jnp.bfloat16)

        tile = min(256, rows)
        for block in range(chunks) if ch is None else [ch]:
            across = pl.ds(pl.multiple_of(block * rows, rows), rows)

            @pl.loop(0, rows // tile)
            def _(t):
                part = pl.ds(pl.multiple_of(t * tile, tile), tile)
                out_ref[part, across] += lax.dot_general(
                    scaled[keep, part, :], held[slot, block], (((1,), (1,)), ((), ())),
                    preferred_element_type=jnp.float32)

    def take_line(at, i):
        line_copy(at, i, q).wait_recv()

        @pl.when(jnp.logical_and(at < z, z < nz - 1))
        def _():
            line_copy(at, i, q + 2).start()

        @pl.when(jnp.logical_and(at > z, z > 0))
        def _():
            line_copy(at, i, q - 2).start()

        @pl.when(paired(at, i))
        def _():
            pair_copy(at, i).start()

        root_sends(2 * at + x, i, x)

    def take_pair(at, i):
        @pl.when(paired(at, i))
        def _():
            along(2 * at + 1 - x, i, 1 - x, q, cross_sem.at[0]).wait_recv()
            root_sends(2 * at + 1 - x, i, 1 - x)

    def multiply_other(at):
        @pl.when(at != buddy)
        def _():
            multiply(2 * at + 1 - x)

    @pl.loop(1, nz)
    def _(k):
        at, before = visit(z, k, nz), visit(z, k - 1, nz)
        for i in range(parts):
            take_line(at, i)
            take_pair(before, i)
            if i == parts // 2 - 1:
                multiply(2 * before + x)

                @pl.when(k >= 2)
                def _():
                    multiply_other(visit(z, jnp.maximum(k - 2, 0), nz))

        @pl.when(jnp.logical_and(k == 1, at_end(z)))
        def _():
            for i in range(parts):
                cross_copy(z, i).start()

    end = visit(z, nz - 1, nz)
    for i in range(parts // 2):
        take_pair(end, i)

    @pl.when(jnp.logical_not(at_end(z)))
    def _():
        for i in range(parts // 2, parts):
            cross_copy(z, i).start()

    multiply(2 * end + x)
    multiply_other(visit(z, nz - 2, nz))

    last, crossed = 2 * end + 1 - x, 2 * buddy + 1 - x
    split = chunks == 2 and nz > 2

    @pl.when(at_end(buddy))
    def _():
        for i in range(parts // 2):
            cross_copy(buddy, i).wait_recv()
            root_sends(crossed, i, 1 - x)

    if split:
        multiply(crossed, turn(0, 1 - x), keep=1)
        multiply(last, turn(0, 1 - x))
    for i in range(parts // 2, parts):
        take_pair(end, i)
    if split:
        multiply(last, turn(parts - 1, 1 - x), again=True)
    else:
        multiply_other(end)
    for i in range(parts // 2, parts):
        cross_copy(buddy, i).wait_recv()
        root_sends(crossed, i, 1 - x)
    if split:
        multiply(crossed, turn(parts - 1, 1 - x), again=True, keep=1)
    else:
        multiply(crossed)

    for i in range(parts):
        @pl.when(jnp.logical_or(i >= parts // 2, at_end(z)))
        def _():
            cross_copy(z, i).wait_send()

    for i in range(parts):
        @pl.when(z > 0)
        def _():
            own_copy(i, q - 2).wait_send()

    @pl.loop(0, nz)
    def _(at):
        sent = jnp.logical_or(jnp.logical_and(at <= z, z < nz - 1), jnp.logical_and(at > z, z > 0))
        for i in range(parts):
            @pl.when(sent)
            def _():
                line_copy(at, i, q).wait_send()

            @pl.when(paired(at, i))
            def _():
                pair_copy(at, i).wait_send()

    @pl.loop(0, nq)
    def _(slot):
        for b in range(bits):
            @pl.when(far % 2 ** (b + 1) == 0)
            def _():
                for sub in range(2):
                    left_copy(left.at[slot], slot, sub, b).wait_send()

    for k in range(1, nq):
        weight_copy(k).wait_send()


def local(nq, nc, configs, weights):
    columns, width = configs.shape
    rows = columns * nc // nq
    chunks = columns // rows
    dma = pltpu.SemaphoreType.DMA
    bits = nc.bit_length() - 1
    return pl.pallas_call(
        functools.partial(kernel, nq, nc),
        out_shape=jax.ShapeDtypeStruct((rows, columns), jnp.float32),
        in_specs=[pl.BlockSpec(memory_space=pl.ANY), pl.BlockSpec(memory_space=pltpu.VMEM)],
        out_specs=pl.BlockSpec(memory_space=pltpu.VMEM),
        scratch_shapes=[
            pltpu.VMEM((nq, chunks, rows, width), jnp.bfloat16),
            pltpu.VMEM((nq, rows, width), jnp.bfloat16),
            pltpu.VMEM((nq, 8, width), jnp.float32),
            pltpu.VMEM((2, rows, width), jnp.bfloat16),
            dma,
            dma((nq, 2 * chunks)),
            dma((nq // 2, 2 * chunks)),
            dma((2 * chunks,)),
            dma((nq // 2, 2 * chunks)),
            dma((2 * chunks,)),
            dma((nq, 2)),
            dma((nq, 2, bits)),
            dma((nq,)),
            dma((nq,)),
        ],
        compiler_params=pltpu.CompilerParams(
            collective_id=0, has_side_effects=True, vmem_limit_bytes=60 * 2**20),
        cost_estimate=pl.CostEstimate(
            flops=2 * rows * columns * width * nq, transcendentals=0,
            bytes_accessed=2 * columns * width + 4 * rows * columns),
    )(configs.reshape(chunks, rows, width), weights)


def solution(mesh):
    return jax.shard_map(
        functools.partial(local, mesh.shape["quad"], mesh.shape["conf"]),
        mesh=mesh,
        in_specs=(P("conf", "quad"), P("quad")),
        out_specs=P("quad", "conf"),
        check_vma=False,
    )
```
